32 devices in a mesh: depth: 4 (over y, core), cam: 8 (over z, x).
Axes of the slice: x: 2, y: 2, z: 4, core: 2. Of those that a mesh axis runs over, the one named last changes fastest.
Arguments:
- block_rays: int32 [4, 8, 32], P('depth', 'cam'), may hold values from -1 to 127, as said below
- block_offsets: int32 [4, 8, 32], P('depth', 'cam'), may hold values from 0 to 255
- view_order: int32 [8], P('cam'), may hold values from 0 to 1
- ray_frames: float32 [8, 6, 128], P('cam'), may hold values from -6 to 6
- target: float32 [8, 128, 64], P('cam'), may hold values from -3 to 3
- enc_freq: float32 [4, 3, 64], P('depth'), may hold values from -32 to 32
- w_in: bfloat16 [4, 128, 256], P('depth'), may hold values from -0.5 to 0.5
- b_in: float32 [4, 256], P('depth'), may hold values from -3 to 3
- w_mid: bfloat16 [4, 256, 256], P('depth'), may hold values from -0.375 to 0.375
- b_mid: float32 [4, 256], P('depth'), may hold values from -3 to 3
- w_feat: bfloat16 [4, 256, 64], P('depth'), may hold values from -0.375 to 0.375
- w_dens: bfloat16 [4, 256], P('depth'), may hold values from -0.375 to 0.375
Outputs:
- pixels: float32 [8, 128, 64], P('cam', 'depth')
- grad_w_in: float32 [4, 128, 256], P('depth', 'cam')
- grad_b_in: float32 [4, 256], P('depth', 'cam')
- grad_w_mid: float32 [4, 256, 256], P('depth', 'cam')
- grad_b_mid: float32 [4, 256], P('depth', 'cam')
- grad_w_feat: float32 [4, 256, 64], P('depth', 'cam')
- grad_w_dens: float32 [4, 256], P('depth', 'cam')
The draws below stay inside these ranges and needn't reach their ends.
Inputs may be any that keep to these rules, and one draw needn't show every extreme that they name: `block_rays`: for each region and batch the used slots come first and hold distinct ray numbers of that batch; later slots hold -1. A region's slots over all batches hold at most 64 ray numbers; in every draw some region holds exactly that many, with one batch in it whose 32 slots are all used.
All inputs are finite; a program needn't handle non-finite values.
Results may differ from the reference program's by a relative error of at most 0.011.
Values sent between devices are 32-bit elements; how exact they have to be, the bound alone decides.
A program may use at most 64 MiB of HBM per device.

```python
import jax
import jax.numpy as jnp
from jax import lax

HID = 256
ENC = 128
FEAT = 64
BLK = 128
OFFS = 256
RAYS = 128
CAP = 32
REGIONS = 4
BATCHES = 8


def region_counts(subkey, is_full):
    quarter = CAP // 4
    subkeys = jax.random.split(subkey, 3)
    ranking = jax.random.permutation(subkeys[0], BATCHES)
    shifts = jax.random.randint(subkeys[1], ((BATCHES - 4) // 2,), -quarter, quarter + 1)
    paired = jnp.stack([quarter + shifts, quarter - shifts], axis=1).reshape(-1)
    values = jnp.concatenate([jnp.full((1,), CAP, jnp.int32), jnp.zeros((3,), jnp.int32), paired.astype(jnp.int32)])
    counts = jnp.zeros((BATCHES,), jnp.int32).at[ranking].set(values)
    ceiling = jnp.where(is_full, CAP, jax.random.randint(subkeys[2], (), quarter, CAP + 1))
    return jnp.minimum(counts, ceiling)


def choose_rays(subkey):
    return jax.random.permutation(subkey, RAYS)[:CAP]


def draw_block_rays(key, part):
    subkeys = jax.random.split(jax.random.fold_in(key, 11), REGIONS + 2)
    full_region = jax.random.randint(subkeys[0], (), 0, REGIONS)
    counts = jax.vmap(region_counts)(subkeys[2:], jnp.arange(REGIONS) == full_region)
    ray_keys = jax.random.split(subkeys[1], REGIONS * BATCHES)
    chosen = jax.vmap(choose_rays)(ray_keys).reshape(REGIONS, BATCHES, CAP)
    occupied = jnp.arange(CAP)[None, None, :] < counts[:, :, None]
    return jnp.where(occupied, chosen, -1).astype(jnp.int32)


def place_ends(result, key, least, high):
    longest = result.shape.index(max(result.shape))
    spots = []
    for shift in (0, 1):
        where = [jax.random.randint(jax.random.fold_in(key, axis), (), 0, length) for axis, length in enumerate(result.shape)]
        where[longest] = (where[longest] + shift) % result.shape[longest]
        spots.append(tuple(where))
    return result.at[spots[0]].set(least).at[spots[1]].set(high)


def level_of(rng, extent, shards, least, top_value):
    def one(position, parts):
        steps = jax.random.uniform(jax.random.fold_in(jax.random.fold_in(rng, 6), position), (parts,), jnp.float32, least / len(shards), top_value / len(shards))
        return jnp.repeat(jnp.exp(steps), extent[position] // parts).reshape((-1,) + (1,) * (len(extent) - position - 1))

    factor_of = one(*shards[0])
    for cut in shards[1:]:
        factor_of = factor_of * one(*cut)
    return factor_of


def scatter_about(stream_key, shape, deviation, bound, cuts=(), kind=jnp.bfloat16):
    entries = jax.random.normal(stream_key, shape, jnp.float32) * deviation
    if len(cuts) > 0:
        entries = level_of(stream_key, shape, cuts, -0.22, 0.18) * entries
    return jnp.clip(entries, min=-bound, max=bound).astype(kind)


def setup_inputs(seed: int = 0) -> dict:
    key_list = jax.random.split(jax.random.key(seed), 13)
    return {
        "block_rays": draw_block_rays(jax.random.fold_in(key_list[12], 71), 0),
        "block_offsets": place_ends(jax.random.randint(key_list[1], (REGIONS, BATCHES, CAP), 0, OFFS), jax.random.fold_in(key_list[1], 1), 0, OFFS - 1).astype(jnp.int32),
        "view_order": place_ends(jax.random.randint(key_list[2], (BATCHES,), 0, 2), jax.random.fold_in(key_list[2], 1), 0, 1).astype(jnp.int32),
        "ray_frames": scatter_about(key_list[3], (BATCHES, 6, RAYS), 1.0, 6.0, ((0, 8),), jnp.float32),
        "target": scatter_about(key_list[4], (BATCHES, RAYS, FEAT), 0.5, 3.0, ((0, 8),), jnp.float32),
        "enc_freq": scatter_about(key_list[5], (REGIONS, 3, ENC // 2), 6.0, 32.0, ((0, 4),), jnp.float32),
        "w_in": scatter_about(key_list[6], (REGIONS, ENC, HID), ENC ** -0.5, 0.5, ((0, 4),)),
        "b_in": scatter_about(key_list[7], (REGIONS, HID), 0.5, 3.0, ((0, 4),), jnp.float32),
        "w_mid": scatter_about(key_list[8], (REGIONS, HID, HID), HID ** -0.5, 0.375, ((0, 4),)),
        "b_mid": scatter_about(key_list[9], (REGIONS, HID), 0.5, 3.0, ((0, 4),), jnp.float32),
        "w_feat": scatter_about(key_list[10], (REGIONS, HID, FEAT), HID ** -0.5, 0.375, ((0, 4),)),
        "w_dens": scatter_about(key_list[11], (REGIONS, HID), HID ** -0.5, 0.375, ((0, 4),)),
    }


step_length = 1.0 / 64.0


def contract_rows(left, right):
    return lax.dot_general(left, right, (((0,), (0,)), ((), ())), preferred_element_type=jnp.float32)


def contract_cols(left, right):
    return lax.dot_general(left, right, (((1,), (1,)), ((), ())), preferred_element_type=jnp.float32)


def strict_upper(samples):
    rows_index = lax.broadcasted_iota(jnp.int32, (samples, samples), 0)
    cols_index = lax.broadcasted_iota(jnp.int32, (samples, samples), 1)
    return (rows_index < cols_index).astype(jnp.float32)


def block_forward(geometry, offsets, frequency, w_in, b_in, w_mid, b_mid, w_feat, w_dens):
    block_count = offsets.shape[0]
    samples = BLK
    positions = (offsets.astype(jnp.float32)[:, None] + jnp.arange(samples, dtype=jnp.float32)[None, :] + 0.5) * step_length
    phases = jnp.zeros((block_count * samples, frequency.shape[1]), jnp.float32)
    for component in range(3):
        coordinate = (geometry[component][:, None] + positions * geometry[component + 3][:, None]).reshape(-1)
        phases = phases + coordinate[:, None] * frequency[component][None, :]
    encoded = jnp.concatenate([jnp.sin(phases), jnp.cos(phases)], axis=1).astype(jnp.bfloat16)
    hidden_one = jax.nn.relu(jnp.dot(encoded, w_in, preferred_element_type=jnp.float32) + b_in).astype(jnp.bfloat16)
    hidden_two = jax.nn.relu(jnp.dot(hidden_one, w_mid, preferred_element_type=jnp.float32) + b_mid).astype(jnp.bfloat16)
    features = jnp.dot(hidden_two, w_feat, preferred_element_type=jnp.float32)
    dens_pre = jnp.dot(hidden_two, w_dens, preferred_element_type=jnp.float32)
    tau_step = (jax.nn.softplus(dens_pre) * step_length).reshape(block_count, samples)
    before = jnp.dot(tau_step, strict_upper(samples), precision=lax.Precision.HIGHEST)
    weights = jnp.exp(-before) * (-jnp.expm1(-tau_step))
    feature_grid = features.reshape(block_count, samples, features.shape[1])
    colour = jnp.einsum("bs,bsf->bf", weights, feature_grid, precision=lax.Precision.HIGHEST)
    through = jnp.exp(-(before[:, -1] + tau_step[:, -1]))
    stored = (encoded, hidden_one, hidden_two, feature_grid, dens_pre, tau_step, before, weights, through)
    return colour, through, stored


def block_backward(stored, d_colour, d_through, w_mid, w_feat, w_dens):
    encoded, hidden_one, hidden_two, feature_grid, dens_pre, tau_step, before, weights, through = stored
    projected = jnp.einsum("bsf,bf->bs", feature_grid, d_colour, precision=lax.Precision.HIGHEST)
    behind = jnp.dot(projected * weights, strict_upper(BLK).T, precision=lax.Precision.HIGHEST)
    d_tau = projected * jnp.exp(-(before + tau_step)) - behind - (d_through * through)[:, None]
    d_pre = ((d_tau * step_length).reshape(-1) * jax.nn.sigmoid(dens_pre)).astype(jnp.bfloat16)
    d_feat = (weights[:, :, None] * d_colour[:, None, :]).reshape(-1, d_colour.shape[1]).astype(jnp.bfloat16)
    grad_feat = contract_rows(hidden_two, d_feat)
    grad_dens = jnp.dot(d_pre, hidden_two, preferred_element_type=jnp.float32)
    d_two = contract_cols(d_feat, w_feat) + d_pre.astype(jnp.float32)[:, None] * w_dens.astype(jnp.float32)[None, :]
    d_two = jnp.where(hidden_two > 0, d_two, 0.0).astype(jnp.bfloat16)
    grad_mid = contract_rows(hidden_one, d_two)
    grad_bmid = jnp.sum(d_two.astype(jnp.float32), axis=0)
    d_one = jnp.where(hidden_one > 0, contract_cols(d_two, w_mid), 0.0).astype(jnp.bfloat16)
    grad_in = contract_rows(encoded, d_one)
    grad_bin = jnp.sum(d_one.astype(jnp.float32), axis=0)
    return grad_in, grad_bin, grad_mid, grad_bmid, grad_feat, grad_dens


def join_pairs(low_pair, high_pair, descending):
    low_colour, low_through = low_pair
    high_colour, high_through = high_pair
    rising = low_colour + low_through[..., None] * high_colour
    falling = high_colour + high_through[..., None] * low_colour
    return jnp.where(descending, falling, rising), low_through * high_through


def region_inputs(region, block_rays, block_offsets, ray_frames, kept_slots):
    capacity = block_rays.shape[2]
    flat_rays = block_rays[region].reshape(-1)
    ranking = jnp.argsort((flat_rays < 0).astype(jnp.int32), stable=True)[:kept_slots].astype(jnp.int32)
    batch_of = (ranking // capacity).astype(jnp.int32)
    ray_number = flat_rays[ranking]
    occupied = ray_number >= 0
    ray_index = jnp.maximum(ray_number, 0).astype(jnp.int32)
    geometry = ray_frames[batch_of, :, ray_index].T
    offsets = block_offsets[region].reshape(-1)[ranking]
    return batch_of, ray_number, occupied, ray_index, geometry, offsets


def reference(block_rays, block_offsets, view_order, ray_frames, target, enc_freq, w_in, b_in, w_mid, b_mid, w_feat, w_dens):
    regions, batches, capacity = block_rays.shape
    ray_total = target.shape[1]
    feature_count = target.shape[2]
    kept_slots = batches * (capacity // 4)
    descending = (view_order == 1)[:, None, None]

    def params_of(region):
        return (enc_freq[region], w_in[region], b_in[region], w_mid[region], b_mid[region], w_feat[region], w_dens[region])

    def forward_region(region):
        batch_of, ray_number, occupied, ray_index, geometry, offsets = region_inputs(region, block_rays, block_offsets, ray_frames, kept_slots)
        colour, through, stored = block_forward(geometry, offsets, *params_of(region))
        slot_ray = jnp.where(occupied, ray_number, ray_total).astype(jnp.int32)
        own_colour = jnp.zeros((batches, ray_total, feature_count), jnp.float32).at[batch_of, slot_ray].add(colour, mode="drop")
        own_through = 1.0 - jnp.zeros((batches, ray_total), jnp.float32).at[batch_of, slot_ray].add(1.0 - through, mode="drop")
        return own_colour, own_through

    own_colour, own_through = lax.map(forward_region, jnp.arange(regions, dtype=jnp.int32))
    identity = (jnp.zeros((batches, ray_total, feature_count), jnp.float32), jnp.ones((batches, ray_total), jnp.float32))

    def rise(running, element):
        return join_pairs(running, element, descending), running

    def fall(running, element):
        return join_pairs(element, running, descending), running

    total, low_pairs = lax.scan(rise, identity, (own_colour, own_through))
    remainder, high_pairs = lax.scan(fall, identity, (own_colour, own_through), reverse=True)
    pixels = total[0]
    grad_pixel = pixels - target
    near_through = jnp.where(descending[None, :, :, 0], high_pairs[1], low_pairs[1])
    far_colour = jnp.where(descending[None], low_pairs[0], high_pairs[0])
    d_colour_ray = near_through[..., None] * grad_pixel[None]
    d_through_ray = near_through * jnp.sum(grad_pixel[None] * far_colour, axis=-1)

    def backward_region(region):
        batch_of, ray_number, occupied, ray_index, geometry, offsets = region_inputs(region, block_rays, block_offsets, ray_frames, kept_slots)
        weights_here = params_of(region)
        colour, through, stored = block_forward(geometry, offsets, *weights_here)
        d_colour = d_colour_ray[region][batch_of, ray_index] * occupied[:, None]
        d_through = d_through_ray[region][batch_of, ray_index] * occupied
        return block_backward(stored, d_colour, d_through, weights_here[3], weights_here[5], weights_here[6])

    gradients = lax.map(backward_region, jnp.arange(regions, dtype=jnp.int32))
    return (pixels, gradients[0], gradients[1], gradients[2], gradients[3], gradients[4], gradients[5])
```

```python
import functools

import jax
import jax.numpy as jnp
from jax import lax
from jax.experimental import pallas as pl
from jax.experimental.pallas import tpu as pltpu
from jax.sharding import PartitionSpec as P

BLK = 128
STEP = 1.0 / 64.0
MESH = pl.DeviceIdType.MESH
HIGH = lax.Precision.HIGHEST
F32 = jnp.float32
BF16 = jnp.bfloat16

TWO_OVER_PI = 0.6366197723675814
HALF_PI_PARTS = (1.5703125, 4.837512969970703125e-4, 7.549789954891882e-8)


def nn(left, right, precision=None):
    return lax.dot_general(
        left, right, (((1,), (0,)), ((), ())), precision=precision, preferred_element_type=F32
    )


def nt(left, right, precision=None):
    return lax.dot_general(
        left, right, (((1,), (1,)), ((), ())), precision=precision, preferred_element_type=F32
    )


def iota(shape, dim):
    return lax.broadcasted_iota(jnp.int32, shape, dim)


def eye(size, dtype):
    return jnp.where(iota((size, size), 0) == iota((size, size), 1), 1.0, 0.0).astype(dtype)


def sin_cos(angle):
    turns = jnp.floor(angle * TWO_OVER_PI + 0.5)
    quadrant = turns.astype(jnp.int32)
    rest = angle
    for part in HALF_PI_PARTS:
        rest = rest - turns * part
    square = rest * rest
    sine = rest + rest * square * (
        -1.6666654611e-1 + square * (8.3321608736e-3 + square * -1.9515295891e-4)
    )
    cosine = (1.0 - 0.5 * square) + square * square * (
        4.166664568298827e-2 + square * (-1.388731625493765e-3 + square * 2.443315711809948e-5)
    )
    odd = (quadrant & 1) == 1
    sin_out = jnp.where(odd, cosine, sine)
    cos_out = jnp.where(odd, sine, cosine)
    sin_out = jnp.where((quadrant & 2) == 2, -sin_out, sin_out)
    cos_out = jnp.where(((quadrant + 1) & 2) == 2, -cos_out, cos_out)
    return sin_out, cos_out


def join(low, high, falling):
    low_colour, low_through = low
    high_colour, high_through = high
    colour = jnp.where(
        falling, high_colour + high_through * low_colour, low_colour + low_through * high_colour
    )
    return colour, low_through * high_through


def send(src, dst, send_sem, recv_sem, axis, peer):
    copy = pltpu.make_async_remote_copy(
        src_ref=src,
        dst_ref=dst,
        send_sem=send_sem,
        recv_sem=recv_sem,
        device_id={axis: peer},
        device_id_type=MESH,
    )
    copy.start()
    return copy


def kernel(
    regions,
    batches,
    rays_ref,
    offsets_ref,
    view_ref,
    frames_ref,
    target_ref,
    freq_ref,
    w_in_ref,
    b_in_ref,
    w_mid_ref,
    b_mid_ref,
    w_feat_ref,
    w_dens_ref,
    pixels_ref,
    grad_in_ref,
    grad_bin_ref,
    grad_mid_ref,
    grad_bmid_ref,
    grad_feat_ref,
    grad_dens_ref,
    geo,
    aim,
    found,
    enc,
    one,
    two,
    heads,
    pre_in,
    pre_mid,
    pre_feat,
    pre_small,
    got_in,
    got_mid,
    got_feat,
    got_small,
    last_in,
    last_mid,
    last_feat,
    last_small,
    geo_send,
    geo_recv,
    aim_send,
    aim_recv,
    cam_send,
    cam_recv,
    depth_send,
    depth_recv,
    pair_send,
    pair_recv,
    last_send,
    last_recv,
):
    region = lax.axis_index("depth")
    batch = lax.axis_index("cam")
    capacity = rays_ref.shape[2]
    slots = capacity // 4
    ray_total, feat = target_ref.shape[1], target_ref.shape[2]
    half_enc = freq_ref.shape[2]
    hidden = w_mid_ref.shape[1]
    cam_peers = [lax.rem(batch + k, batches) for k in range(1, batches)]
    depth_peers = [lax.rem(region + k, regions) for k in range(1, regions)]

    barrier = pltpu.get_barrier_semaphore()
    for peer in cam_peers:
        pl.semaphore_signal(barrier, inc=1, device_id={"cam": peer}, device_id_type=MESH)
    for peer in depth_peers:
        pl.semaphore_signal(barrier, inc=1, device_id={"depth": peer}, device_id_type=MESH)

    rays_row = rays_ref[0]
    falling_here = view_ref[0] == 1
    named = jnp.maximum(rays_row, 0)
    chosen = jnp.where(iota((ray_total, capacity), 0) == named, 1.0, 0.0)
    geo[batch] = jnp.zeros((8, 128), F32)
    geo[batch, 0:6, 0:capacity] = nn(frames_ref[0], chosen, HIGH)
    geo[batch, 6:7, 0:capacity] = offsets_ref[0].astype(F32)
    geo[batch, 7:8, 0:capacity] = rays_row.astype(F32)
    used = jnp.sum(jnp.where(rays_row >= 0, 1.0, 0.0), axis=1, keepdims=True)
    geo[batch, 6:7, capacity : capacity + 1] = used
    geo[batch, 7:8, capacity : capacity + 1] = jnp.where(
        falling_here, jnp.ones((1, 1), F32), jnp.zeros((1, 1), F32)
    )
    diagonal = iota((capacity, capacity), 0) == iota((capacity, capacity), 1)
    rays_column = jnp.sum(jnp.where(diagonal, named.astype(F32), 0.0), axis=1, keepdims=True)
    chosen_rows = jnp.where(
        iota((capacity, ray_total), 1).astype(F32) == rays_column, 1.0, 0.0
    )
    aim[batch] = nn(chosen_rows, target_ref[0], HIGH)

    pl.semaphore_wait(barrier, batches + regions - 2)
    geo_copies = [
        send(geo.at[batch], geo.at[batch], geo_send.at[k], geo_recv.at[k], "cam", peer)
        for k, peer in enumerate(cam_peers)
    ]
    aim_copies = [
        send(aim.at[batch], aim.at[batch], aim_send.at[k], aim_recv.at[k], "cam", peer)
        for k, peer in enumerate(cam_peers)
    ]

    unit = eye(hidden, BF16)
    w_in_t = nt(unit, w_in_ref[0]).astype(BF16)
    w_mid_t = nt(unit, w_mid_ref[0]).astype(BF16)
    w_feat_t = nt(eye(feat, BF16), w_feat_ref[0]).astype(BF16)
    w_dens_row = w_dens_ref[...]
    heads_t = jnp.concatenate(
        [w_feat_t.astype(F32), jnp.broadcast_to(w_dens_row.astype(F32), (16, hidden))], axis=0
    ).astype(BF16)
    unit_f = eye(hidden, F32)
    b_in_col = jnp.sum(unit_f * b_in_ref[...], axis=1, keepdims=True)
    b_mid_col = jnp.sum(unit_f * b_mid_ref[...], axis=1, keepdims=True)
    w_dens_col = jnp.sum(unit_f * w_dens_row.astype(F32), axis=1, keepdims=True)
    unit_e = eye(half_enc, F32)
    freq_cols = [
        jnp.sum(unit_e * freq_ref[0, c : c + 1, :], axis=1, keepdims=True) for c in range(3)
    ]

    for copy in geo_copies:
        copy.wait()

    wanted = (iota((slots, 1), 0) + slots * batch).astype(F32)
    lane = iota((slots, 128), 1).astype(F32)
    start = jnp.zeros((1, 1), F32)
    picked = jnp.zeros((slots, 8), F32)
    batch_of = jnp.zeros((slots, 1), F32)
    falls = jnp.zeros((slots, 1), F32)
    occupied = jnp.zeros((slots, 1), F32)
    picks = []
    for b in range(batches):
        tile = geo[b]
        count = tile[6:7, capacity : capacity + 1]
        inside = jnp.where((wanted >= start) & (wanted < start + count), 1.0, 0.0)
        pick = jnp.where(lane == wanted - start, 1.0, 0.0) * inside
        picked = picked + nt(pick, tile, HIGH)
        picks.append(pick[:, 0:capacity])
        batch_of = batch_of + inside * float(b)
        falls = falls + inside * tile[7:8, capacity : capacity + 1]
        occupied = occupied + inside
        start = start + count
    number = jnp.where(occupied > 0, picked[:, 7:8], -1.0)

    sample = iota((slots, BLK), 1).astype(F32)
    place = (picked[:, 6:7] + sample + 0.5) * STEP
    coords = [picked[:, c : c + 1] + place * picked[:, c + 3 : c + 4] for c in range(3)]
    for s in range(slots):
        phases = freq_cols[0] * coords[0][s : s + 1]
        for c in (1, 2):
            phases = phases + freq_cols[c] * coords[c][s : s + 1]
        sine, cosine = sin_cos(phases)
        enc[0:half_enc, s * BLK : (s + 1) * BLK] = sine.astype(BF16)
        enc[half_enc : 2 * half_enc, s * BLK : (s + 1) * BLK] = cosine.astype(BF16)
    one[...] = jnp.maximum(nn(w_in_t, enc[...]) + b_in_col, 0.0).astype(BF16)
    two[...] = jnp.maximum(nn(w_mid_t, one[...]) + b_mid_col, 0.0).astype(BF16)
    heads[...] = nn(heads_t, two[...])
    dens = jnp.concatenate(
        [heads[feat : feat + 1, s * BLK : (s + 1) * BLK] for s in range(slots)], axis=0
    )
    tau = (jnp.maximum(dens, 0.0) + jnp.log1p(jnp.exp(-jnp.abs(dens)))) * STEP
    ahead = jnp.where(iota((BLK, BLK), 0) < iota((BLK, BLK), 1), 1.0, 0.0)
    before = nn(tau, ahead, HIGH)
    gone = jnp.exp(-tau)
    weights = jnp.exp(-before) * (jnp.tanh(tau * 0.5) * (1.0 + gone))
    left = jnp.exp(-(before + tau))
    through = left[:, BLK - 1 : BLK]
    row = iota((slots, BLK), 0)
    spread = jnp.concatenate(
        [jnp.where(row == s, weights, 0.0) for s in range(slots)], axis=1
    )
    colour = nt(spread, heads[0:feat, :], HIGH)
    found[region, batch] = jnp.concatenate(
        [
            colour,
            1.0 - through,
            number,
            batch_of,
            jnp.zeros((slots, 128 - feat - 3), F32),
        ],
        axis=1,
    )
    cam_copies = [
        send(
            found.at[region, batch],
            found.at[region, batch],
            cam_send.at[k],
            cam_recv.at[k],
            "cam",
            peer,
        )
        for k, peer in enumerate(cam_peers)
    ]
    for copy in cam_copies:
        copy.wait()
    depth_copies = [
        send(
            found.at[region], found.at[region], depth_send.at[k], depth_recv.at[k], "depth", peer
        )
        for k, peer in enumerate(depth_peers)
    ]
    for copy in aim_copies:
        copy.wait()
    aimed = nn(
        jnp.concatenate(picks, axis=1), aim[...].reshape(batches * capacity, feat), HIGH
    )
    share = pixels_ref.shape[1]
    pixel_keys = (
        iota((share, 1), 0) + (batch * ray_total + region * share)
    ).astype(F32)
    own_keys = jnp.where(occupied > 0, batch_of * float(ray_total) + number, -2.0)
    keys = jnp.concatenate([own_keys, pixel_keys], axis=0)
    rows = slots + share
    falling = (
        jnp.concatenate(
            [falls, jnp.where(falling_here, jnp.ones((share, 1), F32), jnp.zeros((share, 1), F32))],
            axis=0,
        )
        > 0.5
    )
    for copy in depth_copies:
        copy.wait()

    key_lane = iota((16, 128), 1)
    key_maker = jnp.where(
        key_lane == feat + 1, 1.0, jnp.where(key_lane == feat + 2, float(ray_total), 0.0)
    ).astype(BF16)
    pairs = []
    for r in range(regions):
        table = found[r].reshape(batches * slots, 128)
        table_keys = nt(key_maker, table.astype(BF16))[0:1, :]
        match = jnp.where(keys == table_keys, 1.0, 0.0)
        own = nn(match, table, HIGH)
        pairs.append((own[:, 0:feat], 1.0 - own[:, feat : feat + 1]))
    empty = (jnp.zeros((rows, feat), F32), jnp.ones((rows, 1), F32))

    def choose(flag, new, old):
        return tuple(jnp.where(flag, n, o) for n, o in zip(new, old))

    low = high = mine = empty
    for r in range(regions):
        low = choose(r < region, join(low, pairs[r], falling), low)
        mine = choose(r == region, pairs[r], mine)
    for r in reversed(range(regions)):
        high = choose(r > region, join(pairs[r], high, falling), high)
    pixels = join(join(low, mine, falling), high, falling)[0]
    pixels_ref[0] = pixels[slots:, :]

    grad_pixel = pixels[0:slots] - aimed
    near = jnp.where(falling, high[1], low[1])[0:slots] * occupied
    far = jnp.where(falling, low[0], high[0])[0:slots]
    d_colour = near * grad_pixel
    d_through = near * jnp.sum(grad_pixel * far, axis=1, keepdims=True)

    projected_all = nn(d_colour, heads[0:feat, :], HIGH)
    projected = jnp.concatenate(
        [projected_all[s : s + 1, s * BLK : (s + 1) * BLK] for s in range(slots)], axis=0
    )
    after = jnp.where(iota((BLK, BLK), 0) > iota((BLK, BLK), 1), 1.0, 0.0)
    behind = nn(projected * weights, after, HIGH)
    d_tau = projected * left - behind - d_through * through
    d_pre = (d_tau * STEP) * (1.0 / (1.0 + jnp.exp(-dens)))
    d_pre_row = jnp.concatenate([d_pre[s : s + 1] for s in range(slots)], axis=1)
    d_colour_t = nt(eye(feat, F32), d_colour, HIGH)
    d_feat = jnp.concatenate(
        [d_colour_t[:, s : s + 1] * weights[s : s + 1] for s in range(slots)], axis=1
    ).astype(BF16)
    samples = slots * BLK
    d_pre_tile = jnp.where(
        iota((16, samples), 0) == 0, jnp.broadcast_to(d_pre_row, (16, samples)), 0.0
    ).astype(BF16)
    d_heads = jnp.concatenate([d_feat, d_pre_tile], axis=0)

    place_lo = lax.rem(batch, 2)
    place_hi = batch // 2
    other_lo = 1 - place_lo
    partner = place_hi * 2 + other_lo
    chunks = (
        (pre_feat, got_feat, last_feat),
        (pre_mid, got_mid, last_mid),
        (pre_in, got_in, last_in),
        (pre_small, got_small, last_small),
    )

    def send_pair(index):
        part, got, unused = chunks[index]
        return send(
            part.at[other_lo], got, pair_send.at[index], pair_recv.at[index], "cam", partner
        )

    feat_rows = grad_feat_ref.shape[1]
    half_rows = feat_rows // 2
    grad = nt(two[...], d_feat)
    for b in range(batches):
        pre_feat[b % 2, b // 2] = jnp.concatenate(
            [
                grad[b * feat_rows : b * feat_rows + half_rows],
                grad[b * feat_rows + half_rows : (b + 1) * feat_rows],
            ],
            axis=1,
        )
    pair_copies = [send_pair(0)]
    grad_dens = nt(d_pre_tile, two[...])[0:1]

    d_two = nn(
        jnp.concatenate(
            [
                w_feat_ref[0].astype(F32),
                jnp.where(iota((hidden, 16), 1) == 0, w_dens_col, 0.0),
            ],
            axis=1,
        ).astype(BF16),
        d_heads,
    )
    d_two = jnp.where(two[...] > 0, d_two, 0.0).astype(BF16)
    mid_rows = grad_mid_ref.shape[1]
    grad = nt(one[...], d_two)
    for b in range(batches):
        pre_mid[b % 2, b // 2] = grad[b * mid_rows : (b + 1) * mid_rows]
    pair_copies.append(send_pair(1))
    ones = jnp.ones((16, samples), BF16)
    grad_bmid = nt(ones, d_two)[0:1]

    d_one = nn(w_mid_ref[0], d_two)
    d_one = jnp.where(one[...] > 0, d_one, 0.0).astype(BF16)
    in_rows = grad_in_ref.shape[1]
    grad = nt(enc[...], d_one)
    for b in range(batches):
        pre_in[b % 2, b // 2] = grad[b * in_rows : (b + 1) * in_rows]
    pair_copies.append(send_pair(2))
    grad_bin = nt(ones, d_one)[0:1]
    lanes = grad_bin_ref.shape[1]
    for b in range(batches):
        cut = slice(b * lanes, (b + 1) * lanes)
        pre_small[b % 2, b // 2] = jnp.concatenate(
            [
                grad_bin[:, cut],
                grad_bmid[:, cut],
                grad_dens[:, cut],
                jnp.zeros((1, 128 - 3 * lanes), F32),
            ],
            axis=1,
        )
    pair_copies.append(send_pair(3))

    spans = batches // 2
    last_copies = []
    for index, (part, got, last) in enumerate(chunks):
        pair_copies[index].wait()
        got[...] = got[...] + part[place_lo]
        for k in range(1, spans):
            to = lax.rem(place_hi + k, spans)
            last_copies.append(
                send(
                    got.at[to],
                    last.at[k - 1],
                    last_send.at[index, k - 1],
                    last_recv.at[index, k - 1],
                    "cam",
                    to * 2 + place_lo,
                )
            )
    totals = []
    for index, (part, got, last) in enumerate(chunks):
        total = got[place_hi]
        for k in range(1, spans):
            last_copies[index * (spans - 1) + k - 1].wait()
            total = total + last[k - 1]
        totals.append(total)
    grad_feat_ref[0, 0:half_rows] = totals[0][:, 0:feat]
    grad_feat_ref[0, half_rows:feat_rows] = totals[0][:, feat : 2 * feat]
    grad_mid_ref[0] = totals[1]
    grad_in_ref[0] = totals[2]
    grad_bin_ref[...] = totals[3][:, 0:lanes]
    grad_bmid_ref[...] = totals[3][:, lanes : 2 * lanes]
    grad_dens_ref[...] = totals[3][:, 2 * lanes : 3 * lanes]


def shards(regions, batches, *args):
    (rays, offsets, view, frames, target, freq, w_in, b_in, w_mid, b_mid, w_feat, w_dens) = args
    capacity = rays.shape[2]
    slots = capacity // 4
    ray_total, feat = target.shape[1:]
    enc, hidden = w_in.shape[1:]
    samples = slots * BLK
    spans = batches // 2
    in_rows, hid_rows = enc // batches, hidden // batches
    parts = {
        "in": (in_rows, hidden),
        "mid": (hid_rows, hidden),
        "feat": (hid_rows // 2, 2 * feat),
        "small": (1, 128),
    }
    vmem = pl.BlockSpec(memory_space=pltpu.VMEM)
    dma = pltpu.SemaphoreType.DMA
    return pl.pallas_call(
        functools.partial(kernel, regions, batches),
        out_shape=(
            jax.ShapeDtypeStruct((1, ray_total // regions, feat), F32),
            jax.ShapeDtypeStruct((1, in_rows, hidden), F32),
            jax.ShapeDtypeStruct((1, hid_rows), F32),
            jax.ShapeDtypeStruct((1, hid_rows, hidden), F32),
            jax.ShapeDtypeStruct((1, hid_rows), F32),
            jax.ShapeDtypeStruct((1, hid_rows, feat), F32),
            jax.ShapeDtypeStruct((1, hid_rows), F32),
        ),
        in_specs=[vmem, vmem, pl.BlockSpec(memory_space=pltpu.SMEM)] + [vmem] * 9,
        out_specs=(vmem,) * 7,
        scratch_shapes=[
            pltpu.VMEM((batches, 8, 128), F32),
            pltpu.VMEM((batches, capacity, feat), F32),
            pltpu.VMEM((regions, batches, slots, 128), F32),
            pltpu.VMEM((enc, samples), BF16),
            pltpu.VMEM((hidden, samples), BF16),
            pltpu.VMEM((hidden, samples), BF16),
            pltpu.VMEM((feat + 16, samples), F32),
        ]
        + [pltpu.VMEM((2, spans) + shape, F32) for shape in parts.values()]
        + [pltpu.VMEM((spans,) + shape, F32) for shape in parts.values()]
        + [pltpu.VMEM((spans - 1,) + shape, F32) for shape in parts.values()]
        + [dma((batches - 1,))] * 6
        + [dma((regions - 1,))] * 2
        + [dma((4,))] * 2
        + [dma((4, spans - 1))] * 2,
        compiler_params=pltpu.CompilerParams(
            collective_id=0, has_side_effects=True, vmem_limit_bytes=40 * 1024 * 1024
        ),
    )(*args)


def solution(mesh):
    placed = (
        P("depth", "cam", None),
        P("depth", "cam", None),
        P("cam"),
        P("cam", None, None),
        P("cam", None, None),
        P("depth", None, None),
        P("depth", None, None),
        P("depth", None),
        P("depth", None, None),
        P("depth", None),
        P("depth", None, None),
        P("depth", None),
    )
    return jax.shard_map(
        functools.partial(shards, mesh.shape["depth"], mesh.shape["cam"]),
        mesh=mesh,
        in_specs=placed,
        out_specs=(
            P("cam", "depth", None),
            P("depth", "cam", None),
            P("depth", "cam"),
            P("depth", "cam", None),
            P("depth", "cam"),
            P("depth", "cam", None),
            P("depth", "cam"),
        ),
        check_vma=False,
    )
```

```python
import functools

import jax
import jax.numpy as jnp
from jax import lax
from jax.experimental import pallas as pl
from jax.experimental.pallas import tpu as pltpu
from jax.sharding import PartitionSpec as P

BLK = 128
STEP = 1.0 / 64.0
MESH = pl.DeviceIdType.MESH
HIGH = lax.Precision.HIGHEST
F32 = jnp.float32
BF16 = jnp.bfloat16

TWO_OVER_PI = 0.6366197723675814
HALF_PI_PARTS = (1.5703125, 4.837512969970703125e-4, 7.549789954891882e-8)


def nn(left, right, precision=None):
    return lax.dot_general(
        left, right, (((1,), (0,)), ((), ())), precision=precision, preferred_element_type=F32
    )


def nt(left, right, precision=None):
    return lax.dot_general(
        left, right, (((1,), (1,)), ((), ())), precision=precision, preferred_element_type=F32
    )


def iota(shape, dim):
    return lax.broadcasted_iota(jnp.int32, shape, dim)


def eye(size, dtype):
    return jnp.where(iota((size, size), 0) == iota((size, size), 1), 1.0, 0.0).astype(dtype)


def sin_cos(angle):
    turns = jnp.floor(angle * TWO_OVER_PI + 0.5)
    quadrant = turns.astype(jnp.int32)
    rest = angle
    for part in HALF_PI_PARTS:
        rest = rest - turns * part
    square = rest * rest
    sine = rest + rest * square * (
        -1.6666654611e-1 + square * (8.3321608736e-3 + square * -1.9515295891e-4)
    )
    cosine = (1.0 - 0.5 * square) + square * square * (
        4.166664568298827e-2 + square * (-1.388731625493765e-3 + square * 2.443315711809948e-5)
    )
    odd = (quadrant & 1) == 1
    sin_out = jnp.where(odd, cosine, sine)
    cos_out = jnp.where(odd, sine, cosine)
    sin_out = jnp.where((quadrant & 2) == 2, -sin_out, sin_out)
    cos_out = jnp.where(((quadrant + 1) & 2) == 2, -cos_out, cos_out)
    return sin_out, cos_out


def pieces(value, count):
    found = []
    for _ in range(count):
        piece = value.astype(BF16)
        found.append(piece.astype(F32))
        value = value - found[-1]
    return found


def stack(parts, axis=0):
    return jnp.concatenate(parts, axis=axis).astype(BF16)


def join(low, high, falling):
    low_colour, low_through = low
    high_colour, high_through = high
    colour = jnp.where(
        falling, high_colour + high_through * low_colour, low_colour + low_through * high_colour
    )
    return colour, low_through * high_through


def send(src, dst, send_sem, recv_sem, axis, peer):
    copy = pltpu.make_async_remote_copy(
        src_ref=src,
        dst_ref=dst,
        send_sem=send_sem,
        recv_sem=recv_sem,
        device_id={axis: peer},
        device_id_type=MESH,
    )
    copy.start()
    return copy


def kernel(
    regions,
    batches,
    rays_ref,
    offsets_ref,
    view_ref,
    frames_ref,
    target_ref,
    freq_ref,
    w_in_ref,
    b_in_ref,
    w_mid_ref,
    b_mid_ref,
    w_feat_ref,
    w_dens_ref,
    packed_ref,
    geo,
    aim,
    found,
    enc,
    one,
    two,
    heads,
    got_in,
    got_mid,
    got_feat,
    last_in,
    last_mid,
    last_feat,
    geo_send,
    geo_recv,
    aim_send,
    aim_recv,
    cam_send,
    cam_recv,
    depth_send,
    depth_recv,
    last_send,
    last_recv,
    loads,
):
    region = lax.axis_index("depth")
    batch = lax.axis_index("cam")
    capacity = rays_ref.shape[2]
    spans = batches // 2
    slots = capacity // 2
    place_lo = lax.rem(batch, 2)
    place_hi = batch // 2
    ray_total, feat = target_ref.shape[2], target_ref.shape[1]
    half_enc = freq_ref.shape[2]
    hidden = w_mid_ref.shape[1]
    cam_peers = [lax.rem(batch + k, batches) for k in range(1, batches)]
    depth_peers = [lax.rem(region + k, regions) for k in range(1, regions)]

    in_rows, hid_rows = 2 * half_enc // batches, hidden // batches

    def kept(part, span, rows):
        low_at, high_at = 2 * span * rows, (2 * span + 1) * rows
        return jnp.where(
            place_lo == 0, part[low_at : low_at + rows], part[high_at : high_at + rows]
        )

    def kept_lanes(row, span):
        low_at, high_at = 2 * span * hid_rows, (2 * span + 1) * hid_rows
        return jnp.where(
            place_lo == 0, row[:, low_at : low_at + hid_rows], row[:, high_at : high_at + hid_rows]
        )

    barrier = pltpu.get_barrier_semaphore()
    for peer in cam_peers:
        pl.semaphore_signal(barrier, inc=1, device_id={"cam": peer}, device_id_type=MESH)
    for peer in depth_peers:
        pl.semaphore_signal(barrier, inc=1, device_id={"depth": peer}, device_id_type=MESH)

    for load in loads[0:4]:
        load.wait()
    rays_row = rays_ref[0]
    falling_here = jnp.where(
        jnp.broadcast_to(view_ref[0], (1, 1)) == 1, 1.0, 0.0
    )
    named = jnp.maximum(rays_row, 0)
    chosen = jnp.where(iota((ray_total, capacity), 0) == named, 1.0, 0.0).astype(BF16)
    frames = jnp.concatenate([frames_ref[:, 0, :], jnp.zeros((2, ray_total), F32)], axis=0)
    placed = nn(stack(pieces(frames, 3)), chosen)
    used = jnp.sum(jnp.where(rays_row >= 0, 1.0, 0.0), axis=1, keepdims=True)
    geo[batch] = jnp.zeros((8, 128), F32)
    geo[batch, :, 0:capacity] = placed[0:8] + placed[8:16] + placed[16:24]
    geo[batch, 6:7, 0:capacity] = offsets_ref[0].astype(F32)
    geo[batch, 7:8, 0:capacity] = rays_row.astype(F32)
    geo[batch, 6:7, capacity : capacity + 1] = used
    geo[batch, 7:8, capacity : capacity + 1] = falling_here

    pl.semaphore_wait(barrier, batches + regions - 2)
    geo_copies = [
        send(geo.at[batch], geo.at[batch], geo_send.at[k], geo_recv.at[k], "cam", peer)
        for k, peer in enumerate(cam_peers)
    ]
    loads[4].wait()
    diagonal = iota((capacity, capacity), 0) == iota((capacity, capacity), 1)
    rays_column = jnp.sum(jnp.where(diagonal, named.astype(F32), 0.0), axis=1, keepdims=True)
    chosen_rows = jnp.where(
        iota((capacity, ray_total), 1).astype(F32) == rays_column, 1.0, 0.0
    ).astype(BF16)
    aim[batch] = nt(chosen_rows, stack(pieces(target_ref[0], 2)))
    aim_copies = [
        send(aim.at[batch], aim.at[batch], aim_send.at[k], aim_recv.at[k], "cam", peer)
        for k, peer in enumerate(cam_peers)
    ]

    for load in loads[5:]:
        load.wait()
    samples = slots * BLK
    unit = eye(hidden, BF16)
    unit_feat = eye(feat, BF16)
    w_in_t = nt(unit, w_in_ref[0]).astype(BF16)
    w_mid_t = nt(unit, w_mid_ref[0]).astype(BF16)
    w_dens_row = w_dens_ref[...].astype(F32)
    heads_t = stack(
        [w_feat_ref[0].astype(F32), jnp.broadcast_to(w_dens_row, (16, hidden))]
    )
    rows_f = pieces(b_in_ref[...], 3) + pieces(b_mid_ref[...], 3)
    columns = nt(unit, stack(rows_f + [w_dens_row] + [jnp.zeros((1, hidden), F32)] * 9))
    b_in_col = columns[:, 0:1] + columns[:, 1:2] + columns[:, 2:3]
    b_mid_col = columns[:, 3:4] + columns[:, 4:5] + columns[:, 5:6]
    w_dens_col = columns[:, 6:7]
    freq = jnp.concatenate([freq_ref[:, 0, :], jnp.zeros((5, half_enc), F32)], axis=0)
    freq_t = nt(eye(half_enc, BF16), stack(pieces(freq, 3)))
    freq_cols = [
        freq_t[:, c : c + 1] + freq_t[:, c + 8 : c + 9] + freq_t[:, c + 16 : c + 17]
        for c in range(3)
    ]
    ones = jnp.ones((16, samples), BF16)

    for copy in geo_copies:
        copy.wait()

    wanted = (iota((slots, 1), 0) + slots * place_hi).astype(F32)
    lane = iota((slots, 128), 1).astype(F32)
    start = jnp.zeros((1, 1), F32)
    batch_of = jnp.zeros((slots, 1), F32)
    falls = jnp.zeros((slots, 1), F32)
    occupied = jnp.zeros((slots, 1), F32)
    picks = []
    tiles = []
    for b in range(batches):
        tile = geo[b]
        count = tile[6:7, capacity : capacity + 1]
        inside = jnp.where((wanted >= start) & (wanted < start + count), 1.0, 0.0)
        pick = jnp.where(lane == wanted - start, 1.0, 0.0) * inside
        tiles.append(stack(pieces(tile, 3)))
        picks.append(pick)
        batch_of = batch_of + inside * float(b)
        falls = falls + inside * tile[7:8, capacity : capacity + 1]
        occupied = occupied + inside
        start = start + count
    triple = nt(stack(picks, 1), jnp.concatenate(tiles, axis=1))
    picked = triple[:, 0:8] + triple[:, 8:16] + triple[:, 16:24]
    number = jnp.where(occupied > 0, picked[:, 7:8], -1.0)

    sample = iota((slots, BLK), 1).astype(F32)
    place = (picked[:, 6:7] + sample + 0.5) * STEP
    coords = [picked[:, c : c + 1] + place * picked[:, c + 3 : c + 4] for c in range(3)]
    for s in range(slots):
        phases = freq_cols[0] * coords[0][s : s + 1]
        for c in (1, 2):
            phases = phases + freq_cols[c] * coords[c][s : s + 1]
        sine, cosine = sin_cos(phases)
        enc[0:half_enc, s * BLK : (s + 1) * BLK] = sine.astype(BF16)
        enc[half_enc : 2 * half_enc, s * BLK : (s + 1) * BLK] = cosine.astype(BF16)
    one[...] = jnp.maximum(nn(w_in_t, enc[...]) + b_in_col, 0.0).astype(BF16)
    two[...] = jnp.maximum(nn(w_mid_t, one[...]) + b_mid_col, 0.0).astype(BF16)
    heads[...] = nn(heads_t, two[...])
    dens = jnp.concatenate(
        [heads[feat : feat + 1, s * BLK : (s + 1) * BLK] for s in range(slots)], axis=0
    )
    tau = (jnp.maximum(dens, 0.0) + jnp.log1p(jnp.exp(-jnp.abs(dens)))) * STEP
    ahead = jnp.where(iota((BLK, BLK), 0) < iota((BLK, BLK), 1), 1.0, 0.0)
    before = nn(stack(pieces(tau, 2)), ahead.astype(BF16))
    before = before[0:slots] + before[slots : 2 * slots]
    gone = jnp.exp(-tau)
    weights = jnp.exp(-before) * (jnp.tanh(tau * 0.5) * (1.0 + gone))
    left = jnp.exp(-(before + tau))
    through = left[:, BLK - 1 : BLK]
    weight_parts = jnp.concatenate(pieces(weights, 2), axis=0)
    row_two = iota((2 * slots, BLK), 0) & (slots - 1)
    spread = stack([jnp.where(row_two == s, weight_parts, 0.0) for s in range(slots)], 1)
    crossed = nt(spread, stack(pieces(heads[0:feat, :], 2)))
    colour = (
        crossed[0:slots, 0:feat]
        + crossed[slots : 2 * slots, 0:feat]
        + crossed[0:slots, feat : 2 * feat]
    )
    found[region, place_hi] = jnp.concatenate(
        [
            colour,
            1.0 - through,
            number,
            batch_of,
            jnp.zeros((slots, 128 - feat - 3), F32),
        ],
        axis=1,
    )
    cam_copies = [
        send(
            found.at[region, place_hi],
            found.at[region, place_hi],
            cam_send.at[k],
            cam_recv.at[k],
            "cam",
            lax.rem(place_hi + k + 1, spans) * 2 + place_lo,
        )
        for k in range(spans - 1)
    ]
    seen = nt(two[...], spread)
    seen = seen[:, 0:slots] + seen[:, slots : 2 * slots]
    heads_rows = stack(
        [
            nt(unit, w_feat_ref[0]),
            jnp.where(iota((hidden, 16), 1) == 0, w_dens_col, 0.0),
        ],
        1,
    )
    one_kept = jnp.concatenate(
        [kept(one, h, hid_rows) for h in range(spans)] + [ones], axis=0
    )
    enc_kept = jnp.concatenate([kept(enc, h, in_rows) for h in range(spans)] + [ones], axis=0)
    for h in range(spans):
        got_in[h, in_rows : in_rows + 8] = jnp.zeros((8, hidden), F32)
    slope = 1.0 / (1.0 + jnp.exp(-dens))
    after = jnp.where(iota((BLK, BLK), 0) > iota((BLK, BLK), 1), 1.0, 0.0).astype(BF16)
    for copy in cam_copies:
        copy.wait()
    depth_copies = [
        send(
            found.at[region], found.at[region], depth_send.at[k], depth_recv.at[k], "depth", peer
        )
        for k, peer in enumerate(depth_peers)
    ]
    for copy in aim_copies:
        copy.wait()
    aimed = nn(
        stack([pick[:, 0:capacity] for pick in picks], 1),
        aim[...].reshape(batches * capacity, 2 * feat).astype(BF16),
    )
    aimed = aimed[:, 0:feat] + aimed[:, feat : 2 * feat]
    share = ray_total // regions
    pixel_keys = (
        iota((share, 1), 0) + (batch * ray_total + region * share)
    ).astype(F32)
    own_keys = jnp.where(occupied > 0, batch_of * float(ray_total) + number, -2.0)
    keys = jnp.concatenate([own_keys, pixel_keys], axis=0)
    rows = slots + share
    falling = (
        jnp.concatenate(
            [falls, jnp.broadcast_to(falling_here, (share, 1))],
            axis=0,
        )
        > 0.5
    )
    for copy in depth_copies:
        copy.wait()

    key_lane = iota((16, 128), 1)
    key_maker = jnp.where(
        key_lane == feat + 1, 1.0, jnp.where(key_lane == feat + 2, float(ray_total), 0.0)
    ).astype(BF16)
    pairs = []
    everyone = spans * slots
    tables = found[...].reshape(regions * everyone, 128)
    table_keys = nt(key_maker, tables.astype(BF16))[0:1, :]
    matches = jnp.where(keys == table_keys, 1.0, 0.0).astype(BF16)
    halves = stack(pieces(tables, 2), 1)
    for r in range(regions):
        cut = slice(r * everyone, (r + 1) * everyone)
        own = nn(matches[:, cut], halves[cut])
        own = own[:, 0:128] + own[:, 128:256]
        pairs.append((own[:, 0:feat], 1.0 - own[:, feat : feat + 1]))
    empty = (jnp.zeros((rows, feat), F32), jnp.ones((rows, 1), F32))

    def choose(flag, new, old):
        return tuple(jnp.where(flag, n, o) for n, o in zip(new, old))

    low = high = mine = empty
    for r in range(regions):
        low = choose(r < region, join(low, pairs[r], falling), low)
        mine = choose(r == region, pairs[r], mine)
    for r in reversed(range(regions)):
        high = choose(r > region, join(pairs[r], high, falling), high)
    pixels = join(join(low, mine, falling), high, falling)[0]
    tops = packed_rows(in_rows, hid_rows, share)
    packed_ref[tops[2] : tops[2] + share, 0:feat] = pixels[slots:, :]

    grad_pixel = pixels[0:slots] - aimed
    near = jnp.where(falling, high[1], low[1])[0:slots] * occupied
    far = jnp.where(falling, low[0], high[0])[0:slots]
    d_colour = near * grad_pixel
    d_through = near * jnp.sum(grad_pixel * far, axis=1, keepdims=True)

    d_colour_t = nt(unit_feat, stack(pieces(d_colour, 2)))
    d_colour_t = d_colour_t[:, 0:slots] + d_colour_t[:, slots : 2 * slots]
    projected = []
    d_feat = []
    for s in range(slots):
        column = jnp.broadcast_to(d_colour_t[:, s : s + 1], (feat, BLK))
        projected.append(
            jnp.sum(heads[0:feat, s * BLK : (s + 1) * BLK] * column, axis=0, keepdims=True)
        )
        d_feat.append(column * weights[s : s + 1])
    projected = jnp.concatenate(projected, axis=0)
    behind = nn(stack(pieces(projected * weights, 2)), after)
    behind = behind[0:slots] + behind[slots : 2 * slots]
    d_tau = projected * left - behind - d_through * through
    d_pre = (d_tau * STEP) * slope
    d_pre_row = jnp.concatenate([d_pre[s : s + 1] for s in range(slots)], axis=1)
    d_feat = stack(d_feat, 1)
    d_pre_tile = jnp.where(
        iota((16, samples), 0) == 0, jnp.broadcast_to(d_pre_row, (16, samples)), 0.0
    ).astype(BF16)
    d_heads = jnp.concatenate([d_feat, d_pre_tile], axis=0)
    grad_dens = nt(d_pre_tile, two[...])[0:1]

    chunks = ((got_feat, last_feat), (got_mid, last_mid), (got_in, last_in))
    last_copies = []

    def send_last(index):
        got, last = chunks[index]
        for k in range(1, spans):
            to = lax.rem(place_hi + k, spans)
            last_copies.append(
                send(
                    got.at[to],
                    last.at[k - 1],
                    last_send.at[index, k - 1],
                    last_recv.at[index, k - 1],
                    "cam",
                    to * 2 + place_lo,
                )
            )

    half_rows = hid_rows // 2
    own_rows = jnp.concatenate([kept(seen, h, hid_rows) for h in range(spans)], axis=0)
    grad = nn(own_rows, d_colour, HIGH)
    for h in range(spans):
        top = h * hid_rows
        got_feat[h] = jnp.concatenate(
            [grad[top : top + half_rows], grad[top + half_rows : top + hid_rows]], axis=1
        )
    send_last(0)

    d_two = nn(heads_rows, d_heads)
    d_two = jnp.where(two[...] > 0, d_two, 0.0).astype(BF16)
    grad = nt(one_kept, d_two)
    for h in range(spans):
        got_mid[h] = grad[h * hid_rows : (h + 1) * hid_rows]
    grad_bmid = grad[spans * hid_rows : spans * hid_rows + 1]
    send_last(1)

    d_one = nn(w_mid_ref[0], d_two)
    d_one = jnp.where(one[...] > 0, d_one, 0.0).astype(BF16)
    grad = nt(enc_kept, d_one)
    grad_bin = grad[spans * in_rows : spans * in_rows + 1]
    for h in range(spans):
        got_in[h, 0:in_rows] = grad[h * in_rows : (h + 1) * in_rows]
        for place, row in enumerate((grad_bin, grad_bmid, grad_dens)):
            got_in[h, in_rows + place : in_rows + place + 1, 0:hid_rows] = kept_lanes(row, h)
    send_last(2)

    totals = []
    for index, (got, last) in enumerate(chunks):
        total = got[place_hi]
        for k in range(1, spans):
            last_copies[index * (spans - 1) + k - 1].wait()
            total = total + last[k - 1]
        totals.append(total)
    packed_ref[tops[2] : tops[2] + half_rows, 128 : 128 + feat] = totals[0][:, 0:feat]
    packed_ref[tops[2] + half_rows : tops[2] + hid_rows, 128 : 128 + feat] = totals[0][
        :, feat : 2 * feat
    ]
    packed_ref[tops[1] : tops[1] + hid_rows, :] = totals[1]
    packed_ref[0:in_rows, :] = totals[2][0:in_rows]
    packed_ref[tops[3] : tops[3] + 3, :] = totals[2][in_rows : in_rows + 3]


def round_up(rows):
    return (rows + 7) // 8 * 8


def packed_rows(in_rows, hid_rows, share):
    mid = round_up(in_rows)
    third = mid + round_up(hid_rows)
    small = third + round_up(max(share, hid_rows))
    return (0, mid, third, small, small + 8)


def entry(regions, batches, *refs):
    sources, local, sems = refs[0:12], refs[-13:-1], refs[-1]
    loads = [pltpu.make_async_copy(sources[i], local[i], sems.at[i]) for i in range(12)]
    for load in loads:
        load.start()
    kernel(regions, batches, *local, *refs[12:-13], loads)


def write_out(packed, *refs):
    outs, staged, sems = refs[0:7], refs[7:14], refs[14]
    pixels, w_in, b_in, w_mid, b_mid, w_feat, w_dens = staged
    share, feat = pixels.shape[1:]
    in_rows, hid_rows = w_in.shape[1], w_mid.shape[1]
    tops = packed_rows(in_rows, hid_rows, share)
    w_mid[0] = packed[tops[1] : tops[1] + hid_rows, :]
    w_in[0] = packed[0:in_rows, :]
    pixels[0] = packed[tops[2] : tops[2] + share, 0:feat]
    w_feat[0] = packed[tops[2] : tops[2] + hid_rows, 128 : 128 + feat]
    for place, ref in enumerate((b_in, b_mid, w_dens)):
        ref[...] = packed[tops[3] + place : tops[3] + place + 1, 0:hid_rows]
    copies = [pltpu.make_async_copy(staged[i], outs[i], sems.at[i]) for i in range(7)]
    for copy in copies:
        copy.start()
    for copy in copies:
        copy.wait()


def shards(regions, batches, *args):
    (rays, offsets, view, frames, target, freq, w_in, b_in, w_mid, b_mid, w_feat, w_dens) = args
    frames = jnp.swapaxes(frames, 0, 1)
    freq = jnp.swapaxes(freq, 0, 1)
    target = jnp.swapaxes(target, 1, 2)
    w_feat = jnp.swapaxes(w_feat, 1, 2)
    args = (rays, offsets, view, frames, target, freq, w_in, b_in, w_mid, b_mid, w_feat, w_dens)
    capacity = rays.shape[2]
    slots = capacity // 2
    feat, ray_total = target.shape[1:]
    enc, hidden = w_in.shape[1:]
    samples = slots * BLK
    spans = batches // 2
    in_rows, hid_rows = enc // batches, hidden // batches
    parts = {
        "in": (in_rows + 8, hidden),
        "mid": (hid_rows, hidden),
        "feat": (hid_rows // 2, 2 * feat),
    }
    vmem = pl.BlockSpec(memory_space=pltpu.VMEM)
    dma = pltpu.SemaphoreType.DMA
    out_shape = (
        jax.ShapeDtypeStruct((1, ray_total // regions, feat), F32),
        jax.ShapeDtypeStruct((1, in_rows, hidden), F32),
        jax.ShapeDtypeStruct((1, hid_rows), F32),
        jax.ShapeDtypeStruct((1, hid_rows, hidden), F32),
        jax.ShapeDtypeStruct((1, hid_rows), F32),
        jax.ShapeDtypeStruct((1, hid_rows, feat), F32),
        jax.ShapeDtypeStruct((1, hid_rows), F32),
    )
    height = packed_rows(in_rows, hid_rows, ray_total // regions)[4]
    packed = pl.pallas_call(
        functools.partial(entry, regions, batches),
        out_shape=jax.ShapeDtypeStruct((height, hidden), F32),
        in_specs=[pl.BlockSpec(memory_space=pl.ANY)] * 12,
        out_specs=vmem,
        scratch_shapes=[
            pltpu.VMEM((batches, 8, 128), F32),
            pltpu.VMEM((batches, capacity, 2 * feat), F32),
            pltpu.VMEM((regions, spans, slots, 128), F32),
            pltpu.VMEM((enc, samples), BF16),
            pltpu.VMEM((hidden, samples), BF16),
            pltpu.VMEM((hidden, samples), BF16),
            pltpu.VMEM((feat + 16, samples), F32),
        ]
        + [pltpu.VMEM((spans,) + shape, F32) for shape in parts.values()]
        + [pltpu.VMEM((spans - 1,) + shape, F32) for shape in parts.values()]
        + [dma((batches - 1,))] * 4
        + [dma((spans - 1,))] * 2
        + [dma((regions - 1,))] * 2
        + [dma((3, spans - 1))] * 2
        + [
            (pltpu.SMEM if arg.ndim == 1 else pltpu.VMEM)(arg.shape, arg.dtype) for arg in args
        ]
        + [dma((12,))],
        compiler_params=pltpu.CompilerParams(
            collective_id=0, has_side_effects=True, vmem_limit_bytes=60 * 1024 * 1024
        ),
    )(*args)
    return pl.pallas_call(
        write_out,
        out_shape=out_shape,
        in_specs=[vmem],
        out_specs=(pl.BlockSpec(memory_space=pl.ANY),) * 7,
        scratch_shapes=[pltpu.VMEM(out.shape, out.dtype) for out in out_shape] + [dma((7,))],
    )(packed)


def solution(mesh):
    placed = (
        P("depth", "cam", None),
        P("depth", "cam", None),
        P("cam"),
        P("cam", None, None),
        P("cam", None, None),
        P("depth", None, None),
        P("depth", None, None),
        P("depth", None),
        P("depth", None, None),
        P("depth", None),
        P("depth", None, None),
        P("depth", None),
    )
    return jax.shard_map(
        functools.partial(shards, mesh.shape["depth"], mesh.shape["cam"]),
        mesh=mesh,
        in_specs=placed,
        out_specs=(
            P("cam", "depth", None),
            P("depth", "cam", None),
            P("depth", "cam"),
            P("depth", "cam", None),
            P("depth", "cam"),
            P("depth", "cam", None),
            P("depth", "cam"),
        ),
        check_vma=False,
    )
```

```python
import functools

import jax
import jax.numpy as jnp
from jax import lax
from jax.experimental import pallas as pl
from jax.experimental.pallas import tpu as pltpu
from jax.sharding import PartitionSpec as P

BLK = 128
STEP = 1.0 / 64.0
MESH = pl.DeviceIdType.MESH
HIGH = lax.Precision.HIGHEST
F32 = jnp.float32
BF16 = jnp.bfloat16

TWO_OVER_PI = 0.6366197723675814
HALF_PI_PARTS = (1.5703125, 4.837512969970703125e-4, 7.549789954891882e-8)


def nn(left, right, precision=None):
    return lax.dot_general(
        left, right, (((1,), (0,)), ((), ())), precision=precision, preferred_element_type=F32
    )


def nt(left, right, precision=None):
    return lax.dot_general(
        left, right, (((1,), (1,)), ((), ())), precision=precision, preferred_element_type=F32
    )


def iota(shape, dim):
    return lax.broadcasted_iota(jnp.int32, shape, dim)


def eye(size, dtype):
    return jnp.where(iota((size, size), 0) == iota((size, size), 1), 1.0, 0.0).astype(dtype)


def sin_cos(angle):
    turns = jnp.floor(angle * TWO_OVER_PI + 0.5)
    quadrant = turns.astype(jnp.int32)
    rest = angle
    for part in HALF_PI_PARTS:
        rest = rest - turns * part
    square = rest * rest
    sine = rest + rest * square * (
        -1.6666654611e-1 + square * (8.3321608736e-3 + square * -1.9515295891e-4)
    )
    cosine = (1.0 - 0.5 * square) + square * square * (
        4.166664568298827e-2 + square * (-1.388731625493765e-3 + square * 2.443315711809948e-5)
    )
    odd = (quadrant & 1) == 1
    sin_out = jnp.where(odd, cosine, sine)
    cos_out = jnp.where(odd, sine, cosine)
    sin_out = jnp.where((quadrant & 2) == 2, -sin_out, sin_out)
    cos_out = jnp.where(((quadrant + 1) & 2) == 2, -cos_out, cos_out)
    return sin_out, cos_out


def pieces(value, count):
    found = []
    for _ in range(count):
        piece = value.astype(BF16)
        found.append(piece.astype(F32))
        value = value - found[-1]
    return found


def stack(parts, axis=0):
    return jnp.concatenate(parts, axis=axis).astype(BF16)


def join(low, high, falling):
    low_colour, low_through = low
    high_colour, high_through = high
    colour = jnp.where(
        falling, high_colour + high_through * low_colour, low_colour + low_through * high_colour
    )
    return colour, low_through * high_through


def send(src, dst, send_sem, recv_sem, axis, peer):
    copy = pltpu.make_async_remote_copy(
        src_ref=src,
        dst_ref=dst,
        send_sem=send_sem,
        recv_sem=recv_sem,
        device_id={axis: peer},
        device_id_type=MESH,
    )
    copy.start()
    return copy


def kernel(
    regions,
    batches,
    rays_ref,
    offsets_ref,
    view_ref,
    frames_ref,
    target_ref,
    freq_ref,
    w_in_ref,
    b_in_ref,
    w_mid_ref,
    b_mid_ref,
    w_feat_ref,
    w_dens_ref,
    packed_ref,
    geo,
    aim,
    found,
    enc,
    one,
    two,
    heads,
    got_in,
    got_mid,
    got_feat,
    last_in,
    last_mid,
    last_feat,
    geo_send,
    geo_recv,
    aim_send,
    aim_recv,
    cam_send,
    cam_recv,
    depth_send,
    depth_recv,
    last_send,
    last_recv,
    loads,
):
    region = lax.axis_index("depth")
    batch = lax.axis_index("cam")
    capacity = rays_ref.shape[2]
    spans = batches // 2
    slots = capacity // 2
    place_lo = lax.rem(batch, 2)
    place_hi = batch // 2
    ray_total, feat = target_ref.shape[2], target_ref.shape[1]
    half_enc = freq_ref.shape[2]
    hidden = w_mid_ref.shape[1]
    cam_peers = [lax.rem(batch + k, batches) for k in range(1, batches)]
    depth_peers = [lax.rem(region + k, regions) for k in range(1, regions)]

    in_rows, hid_rows = 2 * half_enc // batches, hidden // batches

    def kept(part, span, rows):
        low_at, high_at = 2 * span * rows, (2 * span + 1) * rows
        return jnp.where(
            place_lo == 0, part[low_at : low_at + rows], part[high_at : high_at + rows]
        )

    def kept_lanes(row, span):
        low_at, high_at = 2 * span * hid_rows, (2 * span + 1) * hid_rows
        return jnp.where(
            place_lo == 0, row[:, low_at : low_at + hid_rows], row[:, high_at : high_at + hid_rows]
        )

    barrier = pltpu.get_barrier_semaphore()
    for peer in cam_peers:
        pl.semaphore_signal(barrier, inc=1, device_id={"cam": peer}, device_id_type=MESH)
    for peer in depth_peers:
        pl.semaphore_signal(barrier, inc=1, device_id={"depth": peer}, device_id_type=MESH)

    for load in loads[0:4]:
        load.wait()
    rays_row = rays_ref[0]
    falling_here = jnp.where(
        jnp.broadcast_to(view_ref[0], (1, 1)) == 1, 1.0, 0.0
    )
    named = jnp.maximum(rays_row, 0)
    chosen = jnp.where(iota((ray_total, capacity), 0) == named, 1.0, 0.0).astype(BF16)
    frames = jnp.concatenate([frames_ref[:, 0, :], jnp.zeros((2, ray_total), F32)], axis=0)
    placed = nn(stack(pieces(frames, 3)), chosen)
    used = jnp.sum(jnp.where(rays_row >= 0, 1.0, 0.0), axis=1, keepdims=True)
    geo[batch] = jnp.zeros((8, 128), F32)
    geo[batch, :, 0:capacity] = placed[0:8] + placed[8:16] + placed[16:24]
    geo[batch, 6:7, 0:capacity] = offsets_ref[0].astype(F32)
    geo[batch, 7:8, 0:capacity] = rays_row.astype(F32)
    geo[batch, 6:7, capacity : capacity + 1] = used
    geo[batch, 7:8, capacity : capacity + 1] = falling_here

    pl.semaphore_wait(barrier, batches + regions - 2)
    geo_copies = [
        send(geo.at[batch], geo.at[batch], geo_send.at[k], geo_recv.at[k], "cam", peer)
        for k, peer in enumerate(cam_peers)
    ]
    loads[4].wait()
    diagonal = iota((capacity, capacity), 0) == iota((capacity, capacity), 1)
    rays_column = jnp.sum(jnp.where(diagonal, named.astype(F32), 0.0), axis=1, keepdims=True)
    chosen_rows = jnp.where(
        iota((capacity, ray_total), 1).astype(F32) == rays_column, 1.0, 0.0
    ).astype(BF16)
    aim[batch] = nt(chosen_rows, stack(pieces(target_ref[0], 2)))
    aim_copies = [
        send(aim.at[batch], aim.at[batch], aim_send.at[k], aim_recv.at[k], "cam", peer)
        for k, peer in enumerate(cam_peers)
    ]

    for load in loads[5:]:
        load.wait()
    samples = slots * BLK
    unit = eye(hidden, BF16)
    unit_feat = eye(feat, BF16)
    w_in_t = nt(unit, w_in_ref[0]).astype(BF16)
    w_mid_t = nt(unit, w_mid_ref[0]).astype(BF16)
    w_dens_row = w_dens_ref[...].astype(F32)
    heads_t = stack(
        [w_feat_ref[0].astype(F32), jnp.broadcast_to(w_dens_row, (16, hidden))]
    )
    rows_f = pieces(b_in_ref[...], 3) + pieces(b_mid_ref[...], 3)
    columns = nt(unit, stack(rows_f + [w_dens_row] + [jnp.zeros((1, hidden), F32)] * 9))
    b_in_col = columns[:, 0:1] + columns[:, 1:2] + columns[:, 2:3]
    b_mid_col = columns[:, 3:4] + columns[:, 4:5] + columns[:, 5:6]
    w_dens_col = columns[:, 6:7]
    freq = jnp.concatenate([freq_ref[:, 0, :], jnp.zeros((5, half_enc), F32)], axis=0)
    freq_t = nt(eye(half_enc, BF16), stack(pieces(freq, 3)))
    freq_cols = [
        freq_t[:, c : c + 1] + freq_t[:, c + 8 : c + 9] + freq_t[:, c + 16 : c + 17]
        for c in range(3)
    ]
    ones = jnp.ones((16, samples), BF16)

    for copy in geo_copies:
        copy.wait()

    wanted = (iota((slots, 1), 0) + slots * place_hi).astype(F32)
    lane = iota((slots, 128), 1).astype(F32)
    start = jnp.zeros((1, 1), F32)
    batch_of = jnp.zeros((slots, 1), F32)
    falls = jnp.zeros((slots, 1), F32)
    occupied = jnp.zeros((slots, 1), F32)
    picks = []
    tiles = []
    for b in range(batches):
        tile = geo[b]
        count = tile[6:7, capacity : capacity + 1]
        inside = jnp.where((wanted >= start) & (wanted < start + count), 1.0, 0.0)
        pick = jnp.where(lane == wanted - start, 1.0, 0.0) * inside
        tiles.append(stack(pieces(tile, 3)))
        picks.append(pick)
        batch_of = batch_of + inside * float(b)
        falls = falls + inside * tile[7:8, capacity : capacity + 1]
        occupied = occupied + inside
        start = start + count
    triple = nt(stack(picks, 1), jnp.concatenate(tiles, axis=1))
    picked = triple[:, 0:8] + triple[:, 8:16] + triple[:, 16:24]
    number = jnp.where(occupied > 0, picked[:, 7:8], -1.0)

    sample = iota((slots, BLK), 1).astype(F32)
    place = (picked[:, 6:7] + sample + 0.5) * STEP
    coords = [picked[:, c : c + 1] + place * picked[:, c + 3 : c + 4] for c in range(3)]
    for s in range(slots):
        phases = freq_cols[0] * coords[0][s : s + 1]
        for c in (1, 2):
            phases = phases + freq_cols[c] * coords[c][s : s + 1]
        sine, cosine = sin_cos(phases)
        enc[0:half_enc, s * BLK : (s + 1) * BLK] = sine.astype(BF16)
        enc[half_enc : 2 * half_enc, s * BLK : (s + 1) * BLK] = cosine.astype(BF16)
    one[...] = jnp.maximum(nn(w_in_t, enc[...]) + b_in_col, 0.0).astype(BF16)
    two[...] = jnp.maximum(nn(w_mid_t, one[...]) + b_mid_col, 0.0).astype(BF16)
    heads[...] = nn(heads_t, two[...])
    dens = jnp.concatenate(
        [heads[feat : feat + 1, s * BLK : (s + 1) * BLK] for s in range(slots)], axis=0
    )
    tau = (jnp.maximum(dens, 0.0) + jnp.log1p(jnp.exp(-jnp.abs(dens)))) * STEP
    ahead = jnp.where(iota((BLK, BLK), 0) < iota((BLK, BLK), 1), 1.0, 0.0)
    before = nn(stack(pieces(tau, 2)), ahead.astype(BF16))
    before = before[0:slots] + before[slots : 2 * slots]
    gone = jnp.exp(-tau)
    weights = jnp.exp(-before) * (jnp.tanh(tau * 0.5) * (1.0 + gone))
    left = jnp.exp(-(before + tau))
    through = left[:, BLK - 1 : BLK]
    weight_parts = jnp.concatenate(pieces(weights, 2), axis=0)
    row_two = iota((2 * slots, BLK), 0) & (slots - 1)
    spread = stack([jnp.where(row_two == s, weight_parts, 0.0) for s in range(slots)], 1)
    crossed = nt(spread, stack(pieces(heads[0:feat, :], 2)))
    colour = (
        crossed[0:slots, 0:feat]
        + crossed[slots : 2 * slots, 0:feat]
        + crossed[0:slots, feat : 2 * feat]
    )
    found[region, place_hi] = jnp.concatenate(
        [
            colour,
            1.0 - through,
            number,
            batch_of,
            jnp.zeros((slots, 128 - feat - 3), F32),
        ],
        axis=1,
    )
    cam_copies = [
        send(
            found.at[region, place_hi],
            found.at[region, place_hi],
            cam_send.at[k],
            cam_recv.at[k],
            "cam",
            lax.rem(place_hi + k + 1, spans) * 2 + place_lo,
        )
        for k in range(spans - 1)
    ]
    seen = nt(two[...], spread)
    seen = seen[:, 0:slots] + seen[:, slots : 2 * slots]
    heads_rows = stack(
        [
            nt(unit, w_feat_ref[0]),
            jnp.where(iota((hidden, 16), 1) == 0, w_dens_col, 0.0),
        ],
        1,
    )
    one_kept = jnp.concatenate(
        [kept(one, h, hid_rows) for h in range(spans)] + [ones], axis=0
    )
    enc_kept = jnp.concatenate([kept(enc, h, in_rows) for h in range(spans)] + [ones], axis=0)
    for h in range(spans):
        got_in[h, in_rows : in_rows + 8] = jnp.zeros((8, hidden), F32)
    slope = 1.0 / (1.0 + jnp.exp(-dens))
    after = jnp.where(iota((BLK, BLK), 0) > iota((BLK, BLK), 1), 1.0, 0.0).astype(BF16)
    for copy in cam_copies:
        copy.wait()
    depth_copies = [
        send(
            found.at[region], found.at[region], depth_send.at[k], depth_recv.at[k], "depth", peer
        )
        for k, peer in enumerate(depth_peers)
    ]
    for copy in aim_copies:
        copy.wait()
    aimed = nn(
        stack([pick[:, 0:capacity] for pick in picks], 1),
        aim[...].reshape(batches * capacity, 2 * feat).astype(BF16),
    )
    aimed = aimed[:, 0:feat] + aimed[:, feat : 2 * feat]
    share = ray_total // regions
    pixel_keys = (
        iota((share, 1), 0) + (batch * ray_total + region * share)
    ).astype(F32)
    own_keys = jnp.where(occupied > 0, batch_of * float(ray_total) + number, -2.0)
    keys = jnp.concatenate([own_keys, pixel_keys], axis=0)
    rows = slots + share
    falling = (
        jnp.concatenate(
            [falls, jnp.broadcast_to(falling_here, (share, 1))],
            axis=0,
        )
        > 0.5
    )
    for copy in depth_copies:
        copy.wait()

    key_lane = iota((16, 128), 1)
    key_maker = jnp.where(
        key_lane == feat + 1, 1.0, jnp.where(key_lane == feat + 2, float(ray_total), 0.0)
    ).astype(BF16)
    pairs = []
    everyone = spans * slots
    tables = found[...].reshape(regions * everyone, 128)
    table_keys = nt(key_maker, tables.astype(BF16))[0:1, :]
    matches = jnp.where(keys == table_keys, 1.0, 0.0).astype(BF16)
    halves = stack(pieces(tables, 2), 1)
    for r in range(regions):
        cut = slice(r * everyone, (r + 1) * everyone)
        own = nn(matches[:, cut], halves[cut])
        own = own[:, 0:128] + own[:, 128:256]
        pairs.append((own[:, 0:feat], 1.0 - own[:, feat : feat + 1]))
    empty = (jnp.zeros((rows, feat), F32), jnp.ones((rows, 1), F32))

    def choose(flag, new, old):
        return tuple(jnp.where(flag, n, o) for n, o in zip(new, old))

    low = high = mine = empty
    for r in range(regions):
        low = choose(r < region, join(low, pairs[r], falling), low)
        mine = choose(r == region, pairs[r], mine)
    for r in reversed(range(regions)):
        high = choose(r > region, join(pairs[r], high, falling), high)
    pixels = join(join(low, mine, falling), high, falling)[0]
    tops = packed_rows(in_rows, hid_rows, share)
    packed_ref[tops[2] : tops[2] + share, 0:feat] = pixels[slots:, :]

    grad_pixel = pixels[0:slots] - aimed
    near = jnp.where(falling, high[1], low[1])[0:slots] * occupied
    far = jnp.where(falling, low[0], high[0])[0:slots]
    d_colour = near * grad_pixel
    d_through = near * jnp.sum(grad_pixel * far, axis=1, keepdims=True)

    d_colour_t = nt(unit_feat, stack(pieces(d_colour, 2)))
    d_colour_t = d_colour_t[:, 0:slots] + d_colour_t[:, slots : 2 * slots]
    projected = []
    d_feat = []
    for s in range(slots):
        column = jnp.broadcast_to(d_colour_t[:, s : s + 1], (feat, BLK))
        projected.append(
            jnp.sum(heads[0:feat, s * BLK : (s + 1) * BLK] * column, axis=0, keepdims=True)
        )
        d_feat.append(column * weights[s : s + 1])
    projected = jnp.concatenate(projected, axis=0)
    behind = nn(stack(pieces(projected * weights, 2)), after)
    behind = behind[0:slots] + behind[slots : 2 * slots]
    d_tau = projected * left - behind - d_through * through
    d_pre = (d_tau * STEP) * slope
    d_pre_row = jnp.concatenate([d_pre[s : s + 1] for s in range(slots)], axis=1)
    d_feat = stack(d_feat, 1)
    d_pre_tile = jnp.where(
        iota((16, samples), 0) == 0, jnp.broadcast_to(d_pre_row, (16, samples)), 0.0
    ).astype(BF16)
    d_heads = jnp.concatenate([d_feat, d_pre_tile], axis=0)

    chunks = ((got_feat, last_feat), (got_mid, last_mid), (got_in, last_in))
    last_copies = []

    def send_last(index):
        got, last = chunks[index]
        for k in range(1, spans):
            to = lax.rem(place_hi + k, spans)
            last_copies.append(
                send(
                    got.at[to],
                    last.at[k - 1],
                    last_send.at[index, k - 1],
                    last_recv.at[index, k - 1],
                    "cam",
                    to * 2 + place_lo,
                )
            )

    half_rows = hid_rows // 2
    own_rows = jnp.concatenate([kept(seen, h, hid_rows) for h in range(spans)], axis=0)
    grad = nn(own_rows, d_colour, HIGH)
    for h in range(spans):
        top = h * hid_rows
        got_feat[h] = jnp.concatenate(
            [grad[top : top + half_rows], grad[top + half_rows : top + hid_rows]], axis=1
        )
    send_last(0)

    d_two = nn(heads_rows, d_heads)
    d_two = jnp.where(two[...] > 0, d_two, 0.0).astype(BF16)
    grad = nt(one_kept, d_two)
    for h in range(spans):
        got_mid[h] = grad[h * hid_rows : (h + 1) * hid_rows]
    grad_bmid = grad[spans * hid_rows : spans * hid_rows + 1]
    send_last(1)
    grad_dens = nt(d_pre_tile, two[...])[0:1]

    d_one = nn(w_mid_ref[0], d_two)
    d_one = jnp.where(one[...] > 0, d_one, 0.0).astype(BF16)
    grad = nt(enc_kept, d_one)
    grad_bin = grad[spans * in_rows : spans * in_rows + 1]
    for h in range(spans):
        got_in[h, 0:in_rows] = grad[h * in_rows : (h + 1) * in_rows]
        for place, row in enumerate((grad_bin, grad_bmid, grad_dens)):
            got_in[h, in_rows + place : in_rows + place + 1, 0:hid_rows] = kept_lanes(row, h)
    send_last(2)

    totals = []
    for index, (got, last) in enumerate(chunks):
        total = got[place_hi]
        for k in range(1, spans):
            last_copies[index * (spans - 1) + k - 1].wait()
            total = total + last[k - 1]
        totals.append(total)
    packed_ref[tops[2] : tops[2] + half_rows, 128 : 128 + feat] = totals[0][:, 0:feat]
    packed_ref[tops[2] + half_rows : tops[2] + hid_rows, 128 : 128 + feat] = totals[0][
        :, feat : 2 * feat
    ]
    packed_ref[tops[1] : tops[1] + hid_rows, :] = totals[1]
    packed_ref[0:in_rows, :] = totals[2][0:in_rows]
    packed_ref[tops[3] : tops[3] + 3, :] = totals[2][in_rows : in_rows + 3]


def round_up(rows):
    return (rows + 7) // 8 * 8


def packed_rows(in_rows, hid_rows, share):
    mid = round_up(in_rows)
    third = mid + round_up(hid_rows)
    small = third + round_up(max(share, hid_rows))
    return (0, mid, third, small, small + 8)


def entry(regions, batches, *refs):
    sources, local, sems = refs[0:12], refs[-13:-1], refs[-1]
    loads = [pltpu.make_async_copy(sources[i], local[i], sems.at[i]) for i in range(12)]
    for load in loads:
        load.start()
    kernel(regions, batches, *local, *refs[12:-13], loads)


def write_out(packed, *refs):
    outs, staged, sems = refs[0:7], refs[7:14], refs[14]
    pixels, w_in, b_in, w_mid, b_mid, w_feat, w_dens = staged
    share, feat = pixels.shape[1:]
    in_rows, hid_rows = w_in.shape[1], w_mid.shape[1]
    tops = packed_rows(in_rows, hid_rows, share)
    w_mid[0] = packed[tops[1] : tops[1] + hid_rows, :]
    w_in[0] = packed[0:in_rows, :]
    pixels[0] = packed[tops[2] : tops[2] + share, 0:feat]
    w_feat[0] = packed[tops[2] : tops[2] + hid_rows, 128 : 128 + feat]
    for place, ref in enumerate((b_in, b_mid, w_dens)):
        ref[...] = packed[tops[3] + place : tops[3] + place + 1, 0:hid_rows]
    copies = [pltpu.make_async_copy(staged[i], outs[i], sems.at[i]) for i in range(7)]
    for copy in copies:
        copy.start()
    for copy in copies:
        copy.wait()


def shards(regions, batches, *args):
    (rays, offsets, view, frames, target, freq, w_in, b_in, w_mid, b_mid, w_feat, w_dens) = args
    frames = jnp.swapaxes(frames, 0, 1)
    freq = jnp.swapaxes(freq, 0, 1)
    target = jnp.swapaxes(target, 1, 2)
    w_feat = jnp.swapaxes(w_feat, 1, 2)
    args = (rays, offsets, view, frames, target, freq, w_in, b_in, w_mid, b_mid, w_feat, w_dens)
    capacity = rays.shape[2]
    slots = capacity // 2
    feat, ray_total = target.shape[1:]
    enc, hidden = w_in.shape[1:]
    samples = slots * BLK
    spans = batches // 2
    in_rows, hid_rows = enc // batches, hidden // batches
    parts = {
        "in": (in_rows + 8, hidden),
        "mid": (hid_rows, hidden),
        "feat": (hid_rows // 2, 2 * feat),
    }
    vmem = pl.BlockSpec(memory_space=pltpu.VMEM)
    dma = pltpu.SemaphoreType.DMA
    out_shape = (
        jax.ShapeDtypeStruct((1, ray_total // regions, feat), F32),
        jax.ShapeDtypeStruct((1, in_rows, hidden), F32),
        jax.ShapeDtypeStruct((1, hid_rows), F32),
        jax.ShapeDtypeStruct((1, hid_rows, hidden), F32),
        jax.ShapeDtypeStruct((1, hid_rows), F32),
        jax.ShapeDtypeStruct((1, hid_rows, feat), F32),
        jax.ShapeDtypeStruct((1, hid_rows), F32),
    )
    height = packed_rows(in_rows, hid_rows, ray_total // regions)[4]
    packed = pl.pallas_call(
        functools.partial(entry, regions, batches),
        out_shape=jax.ShapeDtypeStruct((height, hidden), F32),
        in_specs=[pl.BlockSpec(memory_space=pl.ANY)] * 12,
        out_specs=vmem,
        scratch_shapes=[
            pltpu.VMEM((batches, 8, 128), F32),
            pltpu.VMEM((batches, capacity, 2 * feat), F32),
            pltpu.VMEM((regions, spans, slots, 128), F32),
            pltpu.VMEM((enc, samples), BF16),
            pltpu.VMEM((hidden, samples), BF16),
            pltpu.VMEM((hidden, samples), BF16),
            pltpu.VMEM((feat + 16, samples), F32),
        ]
        + [pltpu.VMEM((spans,) + shape, F32) for shape in parts.values()]
        + [pltpu.VMEM((spans - 1,) + shape, F32) for shape in parts.values()]
        + [dma((batches - 1,))] * 4
        + [dma((spans - 1,))] * 2
        + [dma((regions - 1,))] * 2
        + [dma((3, spans - 1))] * 2
        + [
            (pltpu.SMEM if arg.ndim == 1 else pltpu.VMEM)(arg.shape, arg.dtype) for arg in args
        ]
        + [dma((12,))],
        compiler_params=pltpu.CompilerParams(
            collective_id=0, has_side_effects=True, vmem_limit_bytes=60 * 1024 * 1024
        ),
    )(*args)
    return pl.pallas_call(
        write_out,
        out_shape=out_shape,
        in_specs=[vmem],
        out_specs=(pl.BlockSpec(memory_space=pl.ANY),) * 7,
        scratch_shapes=[pltpu.VMEM(out.shape, out.dtype) for out in out_shape] + [dma((7,))],
    )(packed)


def solution(mesh):
    placed = (
        P("depth", "cam", None),
        P("depth", "cam", None),
        P("cam"),
        P("cam", None, None),
        P("cam", None, None),
        P("depth", None, None),
        P("depth", None, None),
        P("depth", None),
        P("depth", None, None),
        P("depth", None),
        P("depth", None, None),
        P("depth", None),
    )
    return jax.shard_map(
        functools.partial(shards, mesh.shape["depth"], mesh.shape["cam"]),
        mesh=mesh,
        in_specs=placed,
        out_specs=(
            P("cam", "depth", None),
            P("depth", "cam", None),
            P("depth", "cam"),
            P("depth", "cam", None),
            P("depth", "cam"),
            P("depth", "cam", None),
            P("depth", "cam"),
        ),
        check_vma=False,
    )
```
